32 devices in a mesh: row: 4 (over y, x), col: 8 (over z, core).
Axes of the slice: x: 2, y: 2, z: 4, core: 2. Of those that a mesh axis runs over, the one named last changes fastest.
Arguments:
- ancestor_inverse: float32 [8192, 8192], P('row', 'col'), may hold values from -6 to 6
- panel: float32 [6, 32, 256, 256], P(None, 'row', 'col'), may hold values from -0.09375 to 0.09375
- diag_inverse: float32 [6, 256, 256], replicated, as said below
- structure: int32 [6, 16], replicated, may hold values from 0 to 31, as said below
- block_slot: int32 [32], replicated, may hold values from 0 to 31, as said below
Outputs:
- off_block: float32 [6, 32, 256, 256], P(None, 'row', 'col')
- diag_block: float32 [6, 256, 256], replicated
The draws below stay inside these ranges and needn't reach their ends.
Inputs may be any that keep to these rules, and one draw needn't show every extreme that they name: `structure`: the 16 entries of a supernode are distinct global row blocks. Mapped through block_slot, at most 6 of them fall into any aligned run of 8 storage slots, and for every supernode some run holds exactly 6. `block_slot`: A permutation of the 32 row blocks. `diag_inverse`: lower triangular with a positive diagonal.
All inputs are finite; a program needn't handle non-finite values.
Results may differ from the reference program's by a relative error of at most 0.0001.
Values sent between devices are 32-bit elements; how exact they have to be, the bound alone decides.
No kernel may reach another device: no remote copies, remote signals or barrier semaphores. Data moves between devices by JAX's collectives and lax.ppermute only.
A program may use at most 128 MiB of HBM per device.

```python
import jax
import jax.numpy as jnp
from jax import lax

W = 256
SLOTS_ROW = 8
CAP = 6
S = 6
NB = 32
R = 16


def draw_pattern(key):
    row_groups = NB // SLOTS_ROW
    half_row = SLOTS_ROW // 2
    reach = CAP - half_row
    pair_count = row_groups // 2
    base_key = jax.random.fold_in(key, 101)
    key_shift, key_forced, key_sign, key_score, key_perm = jax.random.split(base_key, 5)
    shift = jax.random.randint(key_shift, (S, pair_count), -reach, reach + 1)
    forced = jax.random.randint(key_forced, (S,), 0, pair_count)
    signs = jax.random.randint(key_sign, (S,), 0, 2) * 2 - 1
    pair_index = jnp.arange(pair_count, dtype=jnp.int32)[None, :]
    shift = jnp.where(pair_index == forced[:, None], reach * signs[:, None], shift)
    counts = jnp.stack([half_row + shift, half_row - shift], axis=-1).reshape(S, row_groups)
    scores = jax.random.randint(key_score, (S, row_groups, SLOTS_ROW), 0, 1 << 20) * SLOTS_ROW + jnp.arange(SLOTS_ROW, dtype=jnp.int32)
    ranks = jnp.sum((scores[:, :, None, :] < scores[:, :, :, None]).astype(jnp.int32), axis=-1)
    picked = (ranks < counts[:, :, None]).astype(jnp.int32).reshape(S, NB)
    position = jnp.cumsum(picked, axis=1) - 1
    onehot = ((position[:, None, :] == jnp.arange(R, dtype=jnp.int32)[None, :, None]) & (picked[:, None, :] == 1)).astype(jnp.int32)
    slot_list = jnp.sum(onehot * jnp.arange(NB, dtype=jnp.int32)[None, None, :], axis=2)
    permuted = jax.random.permutation(key_perm, NB).astype(jnp.int32)
    inverse_perm = jnp.argsort(permuted).astype(jnp.int32)
    structure_ids = jnp.take(inverse_perm, slot_list, axis=0)
    return (structure_ids.astype(jnp.int32), permuted)


def draw_structure(key, part):
    structure_ids, permuted = draw_pattern(key)
    return structure_ids


def draw_block_slot(key, part):
    structure_ids, permuted = draw_pattern(key)
    return permuted


def draw_diag_inverse(key, part):
    key_lower, key_diag = jax.random.split(jax.random.fold_in(key, 7))
    lower = jax.random.normal(key_lower, (S, W, W), jnp.float32) * 0.8 / jnp.sqrt(jnp.float32(W))
    diagonal = jax.random.uniform(key_diag, (S, W, W), jnp.float32, 1.0, 2.0)
    row_ids = jnp.arange(W, dtype=jnp.int32)[:, None]
    col_ids = jnp.arange(W, dtype=jnp.int32)[None, :]
    result = jnp.where(row_ids > col_ids, lower, jnp.where(row_ids == col_ids, diagonal, 0.0))
    return result.astype(jnp.float32)


def steps_of(key, shape, shards, smallest, high):
    def one(dim, shards_of):
        draws = jax.random.uniform(jax.random.fold_in(jax.random.fold_in(key, 6), dim), (shards_of,), jnp.float32, smallest / len(shards), high / len(shards))
        return jnp.repeat(jnp.exp(draws), shape[dim] // shards_of).reshape((-1,) + (1,) * (len(shape) - dim - 1))

    gain = one(*shards[0])
    for cut in shards[1:]:
        gain = gain * one(*cut)
    return gain


def scatter_about(own_key, shape, width, most, cuts=(), held_as=jnp.bfloat16):
    values = width * jax.random.normal(own_key, shape, jnp.float32)
    if cuts:
        values = values * steps_of(own_key, shape, cuts, -0.22, 0.18)
    return jnp.clip(values, -most, most).astype(held_as)


def setup_inputs(seed: int = 0) -> dict:
    splits = jax.random.split(jax.random.key(seed), 6)
    return {
        "ancestor_inverse": scatter_about(splits[0], (NB * W, NB * W), 1.0, 6.0, ((0, 4), (1, 8)), jnp.float32),
        "panel": scatter_about(splits[1], (S, NB, W, W), (R * W) ** -0.5, 0.09375, ((1, 4), (2, 8)), jnp.float32),
        "diag_inverse": draw_diag_inverse(jax.random.fold_in(splits[5], 71), 0),
        "structure": draw_structure(jax.random.fold_in(splits[5], 71), 0),
        "block_slot": draw_block_slot(jax.random.fold_in(splits[5], 71), 0),
    }


def reference(ancestor_inverse, panel, diag_inverse, structure, block_slot):
    highest = lax.Precision.HIGHEST
    slot_ids = jnp.take(block_slot, structure, axis=0).astype(jnp.int32)
    rows_three = ancestor_inverse.reshape(NB, W, NB * W)
    off_list = []
    diag_list = []
    for node in range(S):
        chosen = slot_ids[node]
        normalized = jnp.einsum("qik,kw->qiw", jnp.take(panel[node], chosen, axis=0), diag_inverse[node], precision=highest)
        gathered = jnp.take(rows_three, chosen, axis=0).reshape(R, W, NB, W)
        gathered = jnp.take(gathered, chosen, axis=2).reshape(R * W, R * W)
        flat_panel = normalized.reshape(R * W, W)
        product = jnp.dot(gathered, flat_panel, precision=highest, preferred_element_type=jnp.float32)
        empty = jnp.zeros((NB, W, W), jnp.float32)
        off_list.append(empty.at[chosen].set(-product.reshape(R, W, W)))
        leading = jnp.dot(diag_inverse[node].T, diag_inverse[node], precision=highest, preferred_element_type=jnp.float32)
        correction = jnp.dot(flat_panel.T, product, precision=highest, preferred_element_type=jnp.float32)
        diag_list.append(leading + correction)
    return jnp.stack(off_list), jnp.stack(diag_list)
```

```python
import functools

import jax
import jax.numpy as jnp
from jax import lax
from jax.experimental import pallas as pl
from jax.experimental.pallas import tpu as pltpu
from jax.sharding import PartitionSpec as P

CAP = 6
BATCHES = (2, 2, 2)
F32 = jnp.float32
BF16 = jnp.bfloat16
VMEM_LIMIT = 48 * 1024 * 1024

COUNT, SLOT = 0, 1
FIRST, OWN, OWN_SLOT = SLOT + CAP + 1, SLOT + CAP + 2, SLOT + CAP + 3


def split(x):
    high = x.astype(BF16)
    return high, (x - high.astype(F32)).astype(BF16)


def dot3(a, b, dims):
    dot = functools.partial(lax.dot_general, dimension_numbers=(dims, ((), ())), preferred_element_type=F32)
    return dot(a[0], b[1]) + dot(a[1], b[0]) + dot(a[0], b[0])


def prepare_kernel(n, g, batches, ids, structure, block_slot, panel, dinv, table, packed, *rest):
    pieces, gathered = rest[:-1], rest[-1]
    r, z, c = ids[0], ids[1], ids[2]
    node_count, slot_count, sub, width = panel.shape
    col_slots = slot_count // g
    piece = sub // n
    pos_base = OWN_SLOT + col_slots + 1
    place = [(b, i) for b, count in enumerate(batches) for i in range(count)]
    for s in range(node_count):
        row_bits = jnp.int32(0)
        col_bits = jnp.int32(0)
        for k in range(structure.shape[1]):
            slot = block_slot[structure[s, k]]
            for which in range(2):
                at = slot - (r, z)[which] * slot_count
                inside = (at >= 0) & (at < slot_count)
                bit = jnp.where(inside, jnp.left_shift(jnp.int32(1), jnp.where(inside, at, 0)), 0)
                if which == 0:
                    row_bits = row_bits | bit
                else:
                    col_bits = col_bits | bit
        for k in range(CAP + 1):
            table[s, SLOT + k] = 0
        for k in range(col_slots + 1):
            table[s, OWN_SLOT + k] = 0
        count = jnp.int32(0)
        for q in range(slot_count):
            bit = (row_bits >> q) & 1
            table[s, SLOT + jnp.minimum(count, CAP)] = q
            table[s, pos_base + q] = jnp.where(bit == 1, count, -1)
            count = count + bit
        table[s, COUNT] = count
        first, own = jnp.int32(0), jnp.int32(0)
        for q in range(slot_count):
            bit = (col_bits >> q) & 1
            mine = (q // col_slots) == c
            table[s, OWN_SLOT + own] = q % col_slots
            own = own + jnp.where(mine, bit, 0)
            first = first + jnp.where(q // col_slots < c, bit, 0)
        table[s, FIRST] = first
        table[s, OWN] = own
        for k in range(CAP):
            gathered[pl.ds(k * sub, sub), :] = jnp.where(k < count, panel[s, table[s, SLOT + k]], 0.0)
        rows = dot3(split(gathered[...]), split(dinv[s]), ((1,), (0,))).reshape(CAP, sub, width)
        packed[s] = rows
        b, i = place[s]
        for k in range(n):
            part = rows[:, :piece]
            for j in range(1, n):
                part = jnp.where((r ^ k) == j, rows[:, j * piece : (j + 1) * piece], part)
            pieces[b * n + k][pl.ds(i * CAP, CAP)] = part


def product_kernel(n, g, start, ids, table, ancestor, *rest):
    parts, outs = rest[: n * g], rest[n * g : n * g + g]
    blocks, gathered, acc, sems = rest[n * g + g :]
    r, c = ids[0], ids[2]
    node_count, col_slots = blocks.shape[:2]
    width = gathered.shape[0]
    sub = width // (n * g)
    piece = sub // n

    def copy(i, j, k):
        rows = pl.multiple_of(table[start + i, SLOT + k] * width, width)
        cols = pl.multiple_of(table[start + i, OWN_SLOT + j] * width, width)
        source = ancestor.at[pl.ds(rows, width), pl.ds(cols, width)]
        return pltpu.make_async_copy(source, blocks.at[i, j, k], sems.at[i, j, k])

    def each(i, j, what):
        lax.fori_loop(0, table[start + i, COUNT], lambda k, _: what(i, j, k), None)

    for i in range(node_count):
        lax.fori_loop(0, table[start + i, OWN], lambda j, _: each(i, j, lambda *at: copy(*at).start()), None)

    for i in range(node_count):
        rows, own, first = table[start + i, COUNT], table[start + i, OWN], table[start + i, FIRST]

        def column(j, _):
            entry = i * CAP + first + j
            for jk in range(n):
                for kc in range(g):
                    for zz in range(n):
                        at = zz * (g * sub) + (c ^ kc) * sub + (r ^ jk) * piece
                        gathered[pl.ds(pl.multiple_of(at, piece), piece), :] = parts[jk * g + kc][zz, entry]
            right = split(gathered[...])

            def row(i, j, k):
                copy(i, j, k).wait()
                value = dot3(split(blocks[i, j, k]), right, ((1,), (0,)))
                acc[k] = jnp.where(j == 0, value, acc[k] + value)

            each(i, j, row)

        lax.fori_loop(0, own, column, None)
        for k in range(CAP):
            live = (k < rows) & (own > 0)
            for kc in range(g):
                for zz in range(n):
                    part = acc[k, pl.ds(zz * g * sub, sub), :]
                    for j in range(1, g):
                        part = jnp.where((c ^ kc) == j, acc[k, pl.ds((zz * g + j) * sub, sub), :], part)
                    outs[kc][zz, i * CAP + k] = jnp.where(live, part, 0.0)


def finish_kernel(g, start, ids, table, base, *rest):
    received, (packed, dinv, _, off), rest = rest[: -g - 5], rest[-g - 5 : -g - 1], rest[-g - 1 :]
    diags, product = rest[:g], rest[g]
    c = ids[2]
    s = start + pl.program_id(0)
    slot_count, sub, width = off.shape[1:]
    pos_base = OWN_SLOT + slot_count // g + 1
    total = base[0]
    for more in received:
        total = total + more[0]
    product[...] = total
    for q in range(slot_count):
        at = table[s, pos_base + q]
        block = product[jnp.maximum(at, 0)]
        off[0, q] = jnp.where(at >= 0, -block, 0.0)
    mine = packed[0].reshape(CAP * sub, width)
    dims = ((0,), (0,))
    diag = dot3(split(mine), split(product[...].reshape(CAP * sub, width)), dims)

    def store(value):
        half = width // g
        for kc in range(g):
            part = value[:half]
            for j in range(1, g):
                part = jnp.where((c ^ kc) == j, value[j * half : (j + 1) * half], part)
            diags[kc][0] = part

    store(diag)

    @pl.when((ids[0] == 0) & (ids[1] == 0) & (c == 0))
    def _():
        factor = split(dinv[0])
        store(diag + dot3(factor, factor, dims))


def tree_sum(terms):
    while len(terms) > 1:
        terms = [terms[i] + terms[i + 1] for i in range(0, len(terms), 2)]
    return terms[0]


def pick(arrays, index):
    value = arrays[0]
    for k in range(1, len(arrays)):
        value = jnp.where(index == k, arrays[k], value)
    return value


def after(x):
    return list(lax.optimization_barrier(x))


def body(ancestor, panel, dinv, structure, block_slot):
    n = lax.axis_size("row")
    g = lax.axis_size("col") // n
    r = lax.axis_index("row")
    col = lax.axis_index("col")
    z, c = col // g, col % g
    node_count, slot_count, sub, width = panel.shape
    col_slots = slot_count // g
    piece = sub // n
    ids = jnp.stack([r, z, c]).astype(jnp.int32)
    table_width = OWN_SLOT + col_slots + 1 + slot_count
    batches = BATCHES
    smem = pl.BlockSpec(memory_space=pltpu.SMEM)
    vmem = pl.BlockSpec(memory_space=pltpu.VMEM)
    params = pltpu.CompilerParams(vmem_limit_bytes=VMEM_LIMIT)

    def along_row(x, k):
        return lax.ppermute(x, "row", [(i, i ^ k) for i in range(n)])

    def along_z(x, m):
        return lax.ppermute(x, "col", [(i * g + j, (i ^ m) * g + j) for i in range(n) for j in range(g)])

    def along_core(x, k):
        return lax.ppermute(x, "col", [(i * g + j, i * g + (j ^ k)) for i in range(n) for j in range(g)])

    out = pl.pallas_call(
        functools.partial(prepare_kernel, n, g, batches),
        out_shape=[
            jax.ShapeDtypeStruct((node_count, table_width), jnp.int32),
            jax.ShapeDtypeStruct((node_count, CAP, sub, width), F32),
        ]
        + [jax.ShapeDtypeStruct((count * CAP, piece, width), F32) for count in batches for _ in range(n)],
        in_specs=[smem, smem, smem, vmem, vmem],
        out_specs=[smem] + [vmem] * (1 + n * len(batches)),
        scratch_shapes=[pltpu.VMEM((CAP * sub, width), F32)],
        compiler_params=params,
        name="prepare",
    )(ids, structure, block_slot, panel, dinv)
    table, packed, pieces = out[0], out[1], out[2:]

    starts = [sum(batches[:b]) for b in range(len(batches))]
    halvings = n.bit_length() - 1

    def spread_stage(b, own):
        return [own[0]] + [along_row(own[k], k) for k in range(1, n)]

    def cross_stage(b, spread):
        got = [pick(spread, r ^ z ^ m) for m in range(n)]
        return [got[0]] + [along_z(got[m], m) for m in range(1, n)]

    def plane_stage(b, got):
        run = jnp.stack([pick(got, z ^ i) for i in range(n)])
        return [run] + [along_row(run, k) for k in range(1, n)]

    def product_stage(b, plane):
        start, count = starts[b], batches[b]
        total = count * CAP
        parts = [x if k == 0 else along_core(x, k) for x in plane for k in range(g)]
        outs = pl.pallas_call(
            functools.partial(product_kernel, n, g, start),
            out_shape=[jax.ShapeDtypeStruct((n, total, sub, width), F32)] * g,
            in_specs=[smem, smem, pl.BlockSpec(memory_space=pl.ANY)] + [vmem] * (n * g),
            out_specs=[vmem] * g,
            scratch_shapes=[
                pltpu.VMEM((count, col_slots, CAP, width, width), F32),
                pltpu.VMEM((width, width), F32),
                pltpu.VMEM((CAP, width, width), F32),
                pltpu.SemaphoreType.DMA((count, col_slots, CAP)),
            ],
            compiler_params=params,
            cost_estimate=pl.CostEstimate(flops=1, bytes_accessed=1, transcendentals=0),
            name="product",
        )(ids, table, ancestor, *parts)
        return outs

    def halving_stage(i, b, held):
        if i == 0:
            base = held[0]
            for k in range(1, g):
                base = base + along_core(held[k], k)
            held = [base]
        high, low, bit = n >> (i + 1), 1 << i, (z >> i) & 1
        send = None
        for at, array in enumerate(held):
            inner = low >> at
            split_up = array.reshape((high, 2, inner) + array.shape[1:])
            start_at = (0, 1 - bit, (z >> at) & (inner - 1)) + (0,) * (array.ndim - 1)
            part = lax.dynamic_slice(split_up, start_at, (high, 1, 1) + array.shape[1:])
            part = part.reshape((high,) + array.shape[1:])
            send = part if send is None else send + part
        return held + [along_z(send, low)]

    stages = [spread_stage, cross_stage, plane_stage, product_stage]
    stages += [functools.partial(halving_stage, i) for i in range(halvings)]
    state = [pieces[b * n : (b + 1) * n] for b in range(len(batches))]
    half = width // g
    off = jnp.zeros((node_count, slot_count, sub, width), F32)
    diag_list = []
    for phase in range(len(batches) + len(stages)):
        state = after(state)
        done = phase - len(stages)
        for b in range(len(batches)):
            if 0 <= phase - b < len(stages):
                state[b] = stages[phase - b](b, state[b])
        if done < 0:
            continue
        start, count = starts[done], batches[done]
        of_node = lambda i, ids, table, start=start: (start + i, 0, 0, 0)
        of_dest = lambda at: lambda i, ids, table: (ids[1] >> at, i, 0, 0)
        result = pl.pallas_call(
            functools.partial(finish_kernel, g, start),
            out_shape=[jax.ShapeDtypeStruct(off.shape, F32)]
            + [jax.ShapeDtypeStruct((count, half, width), F32)] * g,
            grid_spec=pltpu.PrefetchScalarGridSpec(
                num_scalar_prefetch=2,
                grid=(count,),
                in_specs=[pl.BlockSpec((1, CAP, sub, width), of_dest(at)) for at in range(halvings + 1)]
                + [
                    pl.BlockSpec((1, CAP, sub, width), of_node),
                    pl.BlockSpec((1, width, width), lambda i, ids, table, start=start: (start + i, 0, 0)),
                    pl.BlockSpec(memory_space=pl.ANY),
                ],
                out_specs=[pl.BlockSpec((1, slot_count, sub, width), of_node)]
                + [pl.BlockSpec((1, half, width), lambda i, ids, table: (i, 0, 0))] * g,
                scratch_shapes=[pltpu.VMEM((CAP, sub, width), F32)],
            ),
            input_output_aliases={5 + halvings: 0},
            compiler_params=params,
            cost_estimate=pl.CostEstimate(flops=1, bytes_accessed=1, transcendentals=0),
            name="finish",
        )(ids, table, *state[done], packed, dinv, off)
        off, shares = result[0], result[1:]
        state[done] = []

        share = shares[0]
        for k in range(1, g):
            share = share + along_core(shares[k], k)
        quarter = half // n
        cut = [lax.dynamic_slice_in_dim(share, (r ^ k) * quarter, quarter, 1) for k in range(n)]
        part = tree_sum([cut[0]] + [along_row(cut[k], k) for k in range(1, n)])
        part = tree_sum([part] + [along_z(part, m) for m in range(1, n)])
        parts = [part] + [along_row(part, k) for k in range(1, n)]
        mine = jnp.concatenate([pick(parts, r ^ j) for j in range(n)], axis=1)
        halves = [mine] + [along_core(mine, k) for k in range(1, g)]
        diag_list.append(jnp.concatenate([pick(halves, c ^ j) for j in range(g)], axis=1))
    return off, jnp.concatenate(diag_list, axis=0)


def solution(mesh):
    in_specs = (P("row", "col"), P(None, "row", "col", None), P(), P(), P())
    out_specs = (P(None, "row", "col", None), P())
    return jax.shard_map(body, mesh=mesh, in_specs=in_specs, out_specs=out_specs, check_vma=False)
```

```python
import functools

import jax
import jax.numpy as jnp
from jax import lax
from jax.experimental import pallas as pl
from jax.experimental.pallas import tpu as pltpu
from jax.sharding import PartitionSpec as P

CAP = 6
BATCHES = (2, 2, 2)
F32 = jnp.float32
BF16 = jnp.bfloat16
VMEM_LIMIT = 60 * 1024 * 1024
PRODUCT_VMEM = 56 * 1024 * 1024

COUNT, SLOT = 0, 1
RUN_COUNT, RUN_SLOT = SLOT + CAP + 1, SLOT + CAP + 2
PLACE = RUN_SLOT + CAP + 1


def split(x):
    high = x.astype(BF16)
    return high, (x - high.astype(F32)).astype(BF16)


def dot3(a, b, dims):
    dot = functools.partial(lax.dot_general, dimension_numbers=(dims, ((), ())), preferred_element_type=F32)
    return dot(a[0], b[1]) + dot(a[1], b[0]) + dot(a[0], b[0])


def prepare_kernel(n, g, groups, ids, structure, block_slot, panel, dinv, table, packed, *rest):
    pieces, gathered = rest[:-1], rest[-1]
    r, z, c = ids[0], ids[1], ids[2]
    node_count, slot_count, sub, width = panel.shape
    piece = sub // n
    place = [(b, i) for b, count in enumerate(groups) for i in range(count)]
    for s in range(node_count):
        row_bits = jnp.int32(0)
        col_bits = jnp.int32(0)
        for k in range(structure.shape[1]):
            slot = block_slot[structure[s, k]]
            for which in range(2):
                at = slot - (r, z)[which] * slot_count
                inside = (at >= 0) & (at < slot_count)
                bit = jnp.where(inside, jnp.left_shift(jnp.int32(1), jnp.where(inside, at, 0)), 0)
                if which == 0:
                    row_bits = row_bits | bit
                else:
                    col_bits = col_bits | bit
        counts = []
        for bits, first in ((row_bits, SLOT), (col_bits, RUN_SLOT)):
            for k in range(CAP + 1):
                table[s, first + k] = 0
            count = jnp.int32(0)
            for q in range(slot_count):
                bit = (bits >> q) & 1
                table[s, first + jnp.minimum(count, CAP)] = q
                if first == SLOT:
                    table[s, PLACE + q] = jnp.where(bit == 1, count, -1)
                count = count + bit
            table[s, first - 1] = count
            counts.append(count)
        count = counts[0]
        for k in range(CAP):
            gathered[pl.ds(k * sub, sub), :] = jnp.where(k < count, panel[s, table[s, SLOT + k]], 0.0)
        rows = dot3(split(gathered[...]), split(dinv[s]), ((1,), (0,))).reshape(CAP, sub, width)
        packed[s] = rows
        b, i = place[s]
        for k in range(n):
            part = rows[:, :piece]
            for j in range(1, n):
                part = jnp.where((r ^ k) == j, rows[:, j * piece : (j + 1) * piece], part)
            pieces[b * n + k][pl.ds(i * CAP, CAP)] = part


def product_kernel(n, g, start, ids, table, *rest):
    sources, parts, (keep, send) = rest[:g], rest[g : g + n * g], rest[g + n * g : g + n * g + 2]
    blocks, run, acc, sems, run_sems = rest[g + n * g + 2 :]
    r, z, c = ids[0], ids[1], ids[2]
    node_count = blocks.shape[0]
    sub = blocks.shape[-2]
    width = acc.shape[-1]
    col_slots = sources[0].shape[-1] // width
    tall = n * sub

    def copy(i, j, k, which):
        slot = table[start + i, RUN_SLOT + j]
        cols = pl.ds(pl.multiple_of((slot % col_slots) * width, width), width)
        q = table[start + i, SLOT + k]
        source = sources[0].at[q, :, c, :, cols] if which == 0 else sources[which].at[q, :, :, cols]
        return pltpu.make_async_copy(source, blocks.at[i, j, k], sems.at[i, j, k])

    def begin(i, j, k):
        owner = table[start + i, RUN_SLOT + j] // col_slots
        for which in range(g):

            @pl.when((c ^ owner) == which)
            def _():
                copy(i, j, k, which).start()

    pieces = [
        pltpu.make_async_copy(parts[jk * g + kc], run.at[:, c ^ kc, r ^ jk], run_sems.at[jk * g + kc])
        for jk in range(n)
        for kc in range(g)
    ]
    for piece in pieces:
        piece.start()
    for i in range(node_count):

        def column_blocks(j, _):
            lax.fori_loop(0, table[start + i, COUNT], lambda k, _: begin(i, j, k), None)

        lax.fori_loop(0, table[start + i, RUN_COUNT], column_blocks, None)
    for piece in pieces:
        piece.wait()

    for i in range(node_count):
        rows, columns = table[start + i, COUNT], table[start + i, RUN_COUNT]

        def column(j, _):
            high, low = split(run[:, :, :, i * CAP + j].reshape(width, width))
            right = jnp.concatenate([high, high, low], axis=0)
            lax.fori_loop(0, rows, lambda k, _: copy(i, j, k, 0).wait(), None)
            for few, many in ((0, 2), (2, 4), (4, CAP)):

                @pl.when((rows > few) & (rows <= many))
                def _():
                    high, low = split(blocks[i, j, :many].reshape(many * tall, width))
                    left = jnp.concatenate([high, low, high], axis=1)
                    value = jnp.dot(left, right, preferred_element_type=F32)
                    at = pl.ds(0, many * tall)
                    acc[at] = jnp.where(j == 0, value, acc[at] + value)

        lax.fori_loop(0, columns, column, None)
        for k in range(CAP):
            live = (k < rows) & (columns > 0)
            for h in range(n // 2):
                even, odd = [
                    jnp.where(live, acc[pl.ds((k * n + 2 * h + bit) * sub, sub)], 0.0) for bit in range(2)
                ]
                keep[h, i * CAP + k] = jnp.where((z & 1) == 0, even, odd)
                send[h, i * CAP + k] = jnp.where((z & 1) == 0, odd, even)


def finish_kernel(g, halvings, start, ids, table, base, *rest):
    received, packed, dinv = rest[:halvings], rest[halvings], rest[halvings + 1]
    off, diags, product = rest[-g - 2], rest[-g - 1 : -1], rest[-1]
    c = ids[2]
    s = start + pl.program_id(0)
    slot_count, sub, width = off.shape[1:]
    total = base[0]
    for more in received:
        total = total + more[0]
    product[...] = total
    for q in range(slot_count):
        at = table[s, PLACE + q]
        block = product[jnp.maximum(at, 0)]
        off[0, q] = jnp.where(at >= 0, -block, 0.0)
    mine = packed[0].reshape(CAP * sub, width)
    dims = ((0,), (0,))
    diag = dot3(split(mine), split(product[...].reshape(CAP * sub, width)), dims)

    def store(value):
        half = width // g
        for kc in range(g):
            part = value[:half]
            for j in range(1, g):
                part = jnp.where((c ^ kc) == j, value[j * half : (j + 1) * half], part)
            diags[kc][0] = part

    store(diag)

    @pl.when((ids[0] == 0) & (ids[1] == 0) & (c == 0))
    def _():
        factor = split(dinv[0])
        store(diag + dot3(factor, factor, dims))


def tree_sum(terms):
    while len(terms) > 1:
        terms = [terms[i] + terms[i + 1] for i in range(0, len(terms), 2)]
    return terms[0]


def pick(arrays, index):
    value = arrays[0]
    for k in range(1, len(arrays)):
        value = jnp.where(index == k, arrays[k], value)
    return value


def after(x):
    return lax.optimization_barrier(x)


def body(ancestor, panel, dinv, structure, block_slot):
    n = lax.axis_size("row")
    g = lax.axis_size("col") // n
    r = lax.axis_index("row")
    col = lax.axis_index("col")
    z, c = col // g, col % g
    node_count, slot_count, sub, width = panel.shape
    col_slots = slot_count // g
    piece = sub // n
    ids = jnp.stack([r, z, c]).astype(jnp.int32)
    table_width = PLACE + slot_count
    batches = BATCHES
    groups = (batches[0], sum(batches[1:]))
    smem = pl.BlockSpec(memory_space=pltpu.SMEM)
    vmem = pl.BlockSpec(memory_space=pltpu.VMEM)
    params = pltpu.CompilerParams(vmem_limit_bytes=VMEM_LIMIT)

    def along_row(x, k):
        return lax.ppermute(x, "row", [(i, i ^ k) for i in range(n)])

    def along_z(x, m):
        return lax.ppermute(x, "col", [(i * g + j, (i ^ m) * g + j) for i in range(n) for j in range(g)])

    def along_core(x, k):
        return lax.ppermute(x, "col", [(i * g + j, i * g + (j ^ k)) for i in range(n) for j in range(g)])

    out = pl.pallas_call(
        functools.partial(prepare_kernel, n, g, groups),
        out_shape=[
            jax.ShapeDtypeStruct((node_count, table_width), jnp.int32),
            jax.ShapeDtypeStruct((node_count, CAP, sub, width), F32),
        ]
        + [jax.ShapeDtypeStruct((count * CAP, piece, width), F32) for count in groups for _ in range(n)],
        in_specs=[smem, smem, smem, vmem, vmem],
        out_specs=[smem] + [vmem] * (1 + n * len(groups)),
        scratch_shapes=[pltpu.VMEM((CAP * sub, width), F32)],
        compiler_params=params,
        name="prepare",
    )(ids, structure, block_slot, panel, dinv)
    table, packed, pieces = out[0], out[1], out[2:]

    starts = [sum(batches[:b]) for b in range(len(batches))]
    halvings = n.bit_length() - 1

    def nothing_before(b, held):
        return held

    def spread_stage(b, own):
        return [own[0]] + [along_row(own[k], k) for k in range(1, n)]

    def before_cross(b, spread):
        return [pick(spread, r ^ z ^ m) for m in range(n)]

    def cross_stage(b, got):
        return [got[0]] + [along_z(got[m], m) for m in range(1, n)]

    def before_plane(b, got):
        return [jnp.stack([pick(got, z ^ i) for i in range(n)])]

    def plane_stage(b, run):
        return run + [along_row(run[0], k) for k in range(1, n)]

    def product_stage(b, plane):
        start, count = starts[b], batches[b]
        total = count * CAP
        parts = [x if k == 0 else along_core(x, k) for x in plane for k in range(g)]
        return pl.pallas_call(
            functools.partial(product_kernel, n, g, start),
            out_shape=[jax.ShapeDtypeStruct((n // 2, total, sub, width), F32)] * 2,
            in_specs=[smem, smem] + [pl.BlockSpec(memory_space=pltpu.HBM)] * (g + n * g),
            out_specs=[vmem] * 2,
            scratch_shapes=[
                pltpu.VMEM((count, CAP, CAP, n, sub, width), F32),
                pltpu.VMEM((n, g, n, total, piece, width), F32),
                pltpu.VMEM((CAP * n * sub, width), F32),
                pltpu.SemaphoreType.DMA((count, CAP, CAP)),
                pltpu.SemaphoreType.DMA((n * g,)),
            ],
            compiler_params=pltpu.CompilerParams(vmem_limit_bytes=PRODUCT_VMEM),
            cost_estimate=pl.CostEstimate(flops=1, bytes_accessed=1, transcendentals=0),
            name="product",
        )(ids, table, blocks, *shared, *parts)

    levels = [1] + list(range(1, halvings + 1))

    def before_halving(i, b, held):
        if i == 0:
            return held
        high, bit = n >> (i + 1), (z >> i) & 1
        send = None
        for level, array in zip(levels, held):
            inner = 1 << (i - level)
            split_up = array.reshape((high, 2, inner) + array.shape[1:])
            start_at = (0, 1 - bit, (z >> level) & (inner - 1)) + (0,) * (array.ndim - 1)
            part = lax.dynamic_slice(split_up, start_at, (high, 1, 1) + array.shape[1:])
            part = part.reshape((high,) + array.shape[1:])
            send = part if send is None else send + part
        return list(held) + [send]

    def halving_stage(i, b, held):
        return list(held[:-1]) + [along_z(held[-1], 1 << i)]

    stages = [
        (before_plane, plane_stage),
        (nothing_before, product_stage),
    ]
    stages += [(functools.partial(before_halving, i), functools.partial(halving_stage, i)) for i in range(halvings)]
    state = [[] for _ in batches]
    cross_stages = [(nothing_before, spread_stage), (before_cross, cross_stage)]
    crossing = [list(pieces[:n]), list(pieces[n:])]
    blocks = ancestor.reshape(slot_count, n, g, sub, col_slots * width)
    shared = [blocks] * (g - 1)
    half = width // g
    quarter = half // n

    def plane_diag(shares):
        share = shares[0]
        for k in range(1, g):
            share = share + along_core(shares[k], k)
        cut = [lax.dynamic_slice_in_dim(share, (r ^ k) * quarter, quarter, 1) for k in range(n)]
        return tree_sum([cut[0]] + [along_row(cut[k], k) for k in range(1, n)])

    def whole_diag(part):
        part = tree_sum([part] + [along_z(part, m) for m in range(1, n)])
        parts = [part] + [along_row(part, k) for k in range(1, n)]
        mine = jnp.concatenate([pick(parts, r ^ j) for j in range(n)], axis=1)
        halves = [mine] + [along_core(mine, k) for k in range(1, g)]
        return jnp.concatenate([pick(halves, c ^ j) for j in range(g)], axis=1)

    off, first_diag = None, None
    last = len(batches) - 1
    for phase in range(2 + len(stages) + last + 1):
        done = phase - 2 - len(stages)
        now = [(b, phase - 2 - b) for b in range(last + 1) if 0 <= phase - 2 - b < len(stages)]
        now_crossing = [(group, phase - group) for group in range(2) if 0 <= phase - group < 2]
        for b, stage in now:
            if stage == 0:
                at = 0 if b == 0 else (starts[b] - batches[0]) * CAP
                state[b] = [array[at : at + batches[b] * CAP] for array in crossing[min(b, 1)]]
            state[b] = stages[stage][0](b, state[b])
        for group, stage in now_crossing:
            crossing[group] = cross_stages[stage][0](group, crossing[group])
        if done < last:
            state, crossing, shared = after((state, crossing, shared))
        for b, stage in now:
            state[b] = stages[stage][1](b, state[b])
        for group, stage in now_crossing:
            crossing[group] = cross_stages[stage][1](group, crossing[group])
        if phase == 0:
            shared = [lax.dynamic_index_in_dim(shared[k - 1], c ^ k, 2, keepdims=False) for k in range(1, g)]
        elif phase == 1:
            shared = [along_core(shared[k - 1], k) for k in range(1, g)]
        if done < 0:
            state, crossing, shared = after((state, crossing, shared))
            continue
        start, count = starts[done], batches[done]
        of_node = lambda i, ids, table, start=start: (start + i, 0, 0, 0)
        of_dest = lambda level: lambda i, ids, table: (ids[1] >> level, i, 0, 0)
        result = pl.pallas_call(
            functools.partial(finish_kernel, g, halvings, start),
            out_shape=[jax.ShapeDtypeStruct((node_count, slot_count, sub, width), F32)]
            + [jax.ShapeDtypeStruct((count, half, width), F32)] * g,
            grid_spec=pltpu.PrefetchScalarGridSpec(
                num_scalar_prefetch=2,
                grid=(count,),
                in_specs=[pl.BlockSpec((1, CAP, sub, width), of_dest(level)) for level in levels]
                + [
                    pl.BlockSpec((1, CAP, sub, width), of_node),
                    pl.BlockSpec((1, width, width), lambda i, ids, table, start=start: (start + i, 0, 0)),
                ]
                + [pl.BlockSpec(memory_space=pl.ANY)] * (off is not None),
                out_specs=[pl.BlockSpec((1, slot_count, sub, width), of_node)]
                + [pl.BlockSpec((1, half, width), lambda i, ids, table: (i, 0, 0))] * g,
                scratch_shapes=[pltpu.VMEM((CAP, sub, width), F32)],
            ),
            input_output_aliases={} if off is None else {5 + halvings: 0},
            compiler_params=params,
            cost_estimate=pl.CostEstimate(flops=1, bytes_accessed=1, transcendentals=0),
            name="finish",
        )(ids, table, *state[done], packed, dinv, *([] if off is None else [off]))
        off, state[done] = result[0], result[1:]
        if done < last - 1:
            state = after(state)
        elif done == last - 1:
            first_diag = plane_diag([jnp.concatenate([held[k] for held in state[:last]]) for k in range(g)])
            state[last], first_diag = after((state[last], first_diag))
    diag = [whole_diag(first_diag)] if last else []
    return off, jnp.concatenate(diag + [whole_diag(plane_diag(state[last]))], axis=0)


def solution(mesh):
    in_specs = (P("row", "col"), P(None, "row", "col", None), P(), P(), P())
    out_specs = (P(None, "row", "col", None), P())
    return jax.shard_map(body, mesh=mesh, in_specs=in_specs, out_specs=out_specs, check_vma=False)
```

```python
import functools

import jax
import jax.numpy as jnp
from jax import lax
from jax.experimental import pallas as pl
from jax.experimental.pallas import tpu as pltpu
from jax.sharding import PartitionSpec as P

CAP = 6
BATCHES = (2, 2, 2)
F32 = jnp.float32
BF16 = jnp.bfloat16
VMEM_LIMIT = 60 * 1024 * 1024
PRODUCT_VMEM = 56 * 1024 * 1024

COUNT, SLOT = 0, 1
RUN_COUNT, RUN_SLOT = SLOT + CAP + 1, SLOT + CAP + 2
PLACE = RUN_SLOT + CAP + 1


def split(x):
    high = x.astype(BF16)
    return high, (x - high.astype(F32)).astype(BF16)


def dot3(a, b, dims):
    left = jnp.concatenate([a[0], a[1], a[0]], axis=dims[0][0])
    right = jnp.concatenate([b[0], b[0], b[1]], axis=dims[1][0])
    return lax.dot_general(left, right, dimension_numbers=(dims, ((), ())), preferred_element_type=F32)


def prepare_kernel(n, g, groups, second, ids, structure, block_slot, panel, dinv, table, packed, line, *rest):
    pieces, gathered = rest[:-1], rest[-1]
    r, z, c = ids[0], ids[1], ids[2]
    node_count, slot_count, sub, width = panel.shape
    piece = sub // n
    place = [(b, i) for b, count in enumerate(groups) for i in range(count)]
    for s in range(node_count):
        row_bits = jnp.int32(0)
        col_bits = jnp.int32(0)
        for k in range(structure.shape[1]):
            slot = block_slot[structure[s, k]]
            for which in range(2):
                at = slot - (r, z)[which] * slot_count
                inside = (at >= 0) & (at < slot_count)
                bit = jnp.where(inside, jnp.left_shift(jnp.int32(1), jnp.where(inside, at, 0)), 0)
                if which == 0:
                    row_bits = row_bits | bit
                else:
                    col_bits = col_bits | bit
        counts = []
        for bits, first in ((row_bits, SLOT), (col_bits, RUN_SLOT)):
            for k in range(CAP + 1):
                table[s, first + k] = 0
            count = jnp.int32(0)
            for q in range(slot_count):
                bit = (bits >> q) & 1
                table[s, first + jnp.minimum(count, CAP)] = q
                if first == SLOT:
                    table[s, PLACE + q] = jnp.where(bit == 1, count, -1)
                count = count + bit
            table[s, first - 1] = count
            counts.append(count)
        count = counts[0]
        for k in range(CAP):
            gathered[pl.ds(k * sub, sub), :] = jnp.where(k < count, panel[s, table[s, SLOT + k]], 0.0)
        rows = dot3(split(gathered[...]), split(dinv[s]), ((1,), (0,))).reshape(CAP, sub, width)
        packed[s] = rows
        if s in second:
            line[pl.ds((s - second[0]) * CAP, CAP)] = rows
        b, i = place[s]
        for k in range(n):
            part = rows[:, :piece]
            for j in range(1, n):
                part = jnp.where((r ^ k) == j, rows[:, j * piece : (j + 1) * piece], part)
            pieces[b * n + k][pl.ds(i * CAP, CAP)] = part


def product_kernel(n, g, start, ids, table, *rest):
    sources, near, far, (keep, send) = rest[:g], rest[g : g + n], rest[g + n : 2 * g + n - 1], rest[2 * g + n - 1 : 2 * g + n + 1]
    blocks, run, acc, sems, run_sems = rest[2 * g + n + 1 :]
    r, z, c = ids[0], ids[1], ids[2]
    node_count = blocks.shape[0]
    sub = blocks.shape[-2]
    width = acc.shape[-1]
    col_slots = sources[0].shape[-1] // width
    tall = n * sub

    def copy(i, j, k, which):
        slot = table[start + i, RUN_SLOT + j]
        cols = pl.ds(pl.multiple_of((slot % col_slots) * width, width), width)
        q = table[start + i, SLOT + k]
        source = sources[0].at[q, :, c, :, cols] if which == 0 else sources[which].at[q, :, :, cols]
        return pltpu.make_async_copy(source, blocks.at[i, j, k], sems.at[i, j, k])

    def begin(i, j, k):
        owner = table[start + i, RUN_SLOT + j] // col_slots
        for which in range(g):

            @pl.when((c ^ owner) == which)
            def _():
                copy(i, j, k, which).start()

    pieces = [
        pltpu.make_async_copy(far[kc - 1].at[jk] if kc else near[jk], run.at[:, c ^ kc, r ^ jk], run_sems.at[jk * g + kc])
        for jk in range(n)
        for kc in range(g)
    ]
    for piece in pieces:
        piece.start()
    for i in range(node_count):

        def column_blocks(j, _):
            lax.fori_loop(0, table[start + i, COUNT], lambda k, _: begin(i, j, k), None)

        lax.fori_loop(0, table[start + i, RUN_COUNT], column_blocks, None)
    for piece in pieces:
        piece.wait()

    for i in range(node_count):
        rows, columns = table[start + i, COUNT], table[start + i, RUN_COUNT]

        def column(j, _):
            high, low = split(run[:, :, :, i * CAP + j].reshape(width, width))
            right = jnp.concatenate([high, high, low], axis=0)
            lax.fori_loop(0, rows, lambda k, _: copy(i, j, k, 0).wait(), None)
            for few, many in ((0, 2), (2, 4), (4, CAP)):

                @pl.when((rows > few) & (rows <= many))
                def _():
                    high, low = split(blocks[i, j, :many].reshape(many * tall, width))
                    left = jnp.concatenate([high, low, high], axis=1)
                    value = jnp.dot(left, right, preferred_element_type=F32)
                    at = pl.ds(0, many * tall)
                    acc[at] = jnp.where(j == 0, value, acc[at] + value)

        lax.fori_loop(0, columns, column, None)
        for k in range(CAP):
            live = (k < rows) & (columns > 0)
            for h in range(n // 2):
                even, odd = [
                    jnp.where(live, acc[pl.ds((k * n + 2 * h + bit) * sub, sub)], 0.0) for bit in range(2)
                ]
                keep[h, i * CAP + k] = jnp.where((z & 1) == 0, even, odd)
                send[h, i * CAP + k] = jnp.where((z & 1) == 0, odd, even)


def finish_kernel(g, halvings, with_off, with_diag, start, ids, table, base, *rest):
    received, packed, dinv = rest[:halvings], rest[halvings], rest[halvings + 1]
    product, outs = rest[-1], rest[-1 - with_off - g * with_diag : -1]
    s = start + pl.program_id(0)
    total = base[0]
    for more in received:
        total = total + more[0]
    product[...] = total
    sub, width = product.shape[1:]
    if with_off:
        off = outs[0]
        for q in range(off.shape[1]):
            at = table[s, PLACE + q]
            block = product[jnp.maximum(at, 0)]
            off[0, q] = jnp.where(at >= 0, -block, 0.0)
    if not with_diag:
        return
    mine = packed[0].reshape(CAP * sub, width)
    diag = dot3(split(mine), split(product[...].reshape(CAP * sub, width)), ((0,), (0,)))
    store_shares(diag, dinv, g, ids, outs[with_off:])


def store_shares(diag, dinv, g, ids, shares):
    def store(value):
        half = value.shape[0] // g
        for kc in range(g):
            part = value[:half]
            for j in range(1, g):
                part = jnp.where((ids[2] ^ kc) == j, value[j * half : (j + 1) * half], part)
            shares[kc][0] = part

    store(diag)

    @pl.when((ids[0] == 0) & (ids[1] == 0) & (ids[2] == 0))
    def _():
        factor = split(dinv[0])
        store(diag + dot3(factor, factor, ((0,), (0,))))


def last_diag_kernel(g, halvings, ids, base, *rest):
    received, packed, dinv, shares = rest[:halvings], rest[halvings], rest[halvings + 1], rest[halvings + 2 :]
    width = dinv.shape[-1]
    half = width // g
    dims = ((0,), (0,))
    for i in range(dinv.shape[0]):
        at = pl.ds(i * CAP, CAP)
        total = base[0, at]
        for more in received:
            total = total + more[0, at]
        diag = dot3(split(packed[i].reshape(-1, width)), split(total.reshape(-1, width)), dims)

        def store(value):
            for kc in range(g):
                part = value[:half]
                for j in range(1, g):
                    part = jnp.where((ids[2] ^ kc) == j, value[j * half : (j + 1) * half], part)
                shares[kc][i] = part

        store(diag)

        @pl.when((ids[0] == 0) & (ids[1] == 0) & (ids[2] == 0))
        def _():
            factor = split(dinv[i])
            store(diag + dot3(factor, factor, dims))


def tree_sum(terms):
    while len(terms) > 1:
        terms = [terms[i] + terms[i + 1] for i in range(0, len(terms), 2)]
    return terms[0]


def pick(arrays, index):
    value = arrays[0]
    for k in range(1, len(arrays)):
        value = jnp.where(index == k, arrays[k], value)
    return value


def after(x):
    return lax.optimization_barrier(x)


def body(ancestor, panel, dinv, structure, block_slot):
    n = lax.axis_size("row")
    g = lax.axis_size("col") // n
    r = lax.axis_index("row")
    col = lax.axis_index("col")
    z, c = col // g, col % g
    node_count, slot_count, sub, width = panel.shape
    col_slots = slot_count // g
    piece = sub // n
    ids = jnp.stack([r, z, c]).astype(jnp.int32)
    table_width = PLACE + slot_count
    batches = BATCHES
    groups = (batches[0], sum(batches[1:]))
    smem = pl.BlockSpec(memory_space=pltpu.SMEM)
    vmem = pl.BlockSpec(memory_space=pltpu.VMEM)
    params = pltpu.CompilerParams(vmem_limit_bytes=VMEM_LIMIT)

    def along_row(x, k):
        return lax.ppermute(x, "row", [(i, i ^ k) for i in range(n)])

    def along_z(x, m):
        return lax.ppermute(x, "col", [(i * g + j, (i ^ m) * g + j) for i in range(n) for j in range(g)])

    def along_core(x, k):
        return lax.ppermute(x, "col", [(i * g + j, i * g + (j ^ k)) for i in range(n) for j in range(g)])

    out = pl.pallas_call(
        functools.partial(prepare_kernel, n, g, groups, range(batches[0], batches[0] + batches[1])),
        out_shape=[
            jax.ShapeDtypeStruct((node_count, table_width), jnp.int32),
            jax.ShapeDtypeStruct((node_count, CAP, sub, width), F32),
            jax.ShapeDtypeStruct((batches[1] * CAP, sub, width), F32),
        ]
        + [jax.ShapeDtypeStruct((count * CAP, piece, width), F32) for count in groups for _ in range(n)],
        in_specs=[smem, smem, smem, vmem, vmem],
        out_specs=[smem] + [vmem] * (2 + n * len(groups)),
        scratch_shapes=[pltpu.VMEM((CAP * sub, width), F32)],
        compiler_params=params,
        name="prepare",
    )(ids, structure, block_slot, panel, dinv)
    table, packed, line, pieces = out[0], out[1], [out[2]], out[3:]

    starts = [sum(batches[:b]) for b in range(len(batches))]
    halvings = n.bit_length() - 1

    def nothing_before(b, held):
        return held

    def spread_stage(b, own):
        return [own[0]] + [along_row(own[k], k) for k in range(1, n)]

    def before_cross(b, spread):
        return [pick(spread, r ^ z ^ m) for m in range(n)]

    def cross_stage(b, got):
        return [got[0]] + [along_z(got[m], m) for m in range(1, n)]

    def before_plane(b, got):
        return [jnp.stack([pick(got, z ^ i) for i in range(n)])]

    def plane_stage(b, run):
        return run + [along_row(run[0], k) for k in range(1, n)]

    def product_stage(b, plane):
        start, count = starts[b], batches[b]
        total = count * CAP
        parts = list(plane) + [along_core(jnp.stack(plane), k) for k in range(1, g)]
        return pl.pallas_call(
            functools.partial(product_kernel, n, g, start),
            out_shape=[jax.ShapeDtypeStruct((n // 2, total, sub, width), F32)] * 2,
            in_specs=[smem, smem] + [pl.BlockSpec(memory_space=pltpu.HBM)] * (2 * g + n - 1),
            out_specs=[vmem] * 2,
            scratch_shapes=[
                pltpu.VMEM((count, CAP, CAP, n, sub, width), F32),
                pltpu.VMEM((n, g, n, total, piece, width), F32),
                pltpu.VMEM((CAP * n * sub, width), F32),
                pltpu.SemaphoreType.DMA((count, CAP, CAP)),
                pltpu.SemaphoreType.DMA((n * g,)),
            ],
            compiler_params=pltpu.CompilerParams(vmem_limit_bytes=PRODUCT_VMEM),
            cost_estimate=pl.CostEstimate(flops=1, bytes_accessed=1, transcendentals=0),
            name="product",
        )(ids, table, blocks, *shared, *parts)

    levels = [1] + list(range(1, halvings + 1))

    def before_halving(i, b, held):
        if i == 0:
            return held
        high, bit = n >> (i + 1), (z >> i) & 1
        send = None
        for level, array in zip(levels, held):
            inner = 1 << (i - level)
            split_up = array.reshape((high, 2, inner) + array.shape[1:])
            start_at = (0, 1 - bit, (z >> level) & (inner - 1)) + (0,) * (array.ndim - 1)
            part = lax.dynamic_slice(split_up, start_at, (high, 1, 1) + array.shape[1:])
            part = part.reshape((high,) + array.shape[1:])
            send = part if send is None else send + part
        return list(held) + [send]

    def halving_stage(i, b, held):
        return list(held[:-1]) + [along_z(held[-1], 1 << i)]

    stages = [
        (before_plane, plane_stage),
        (nothing_before, product_stage),
    ]
    stages += [(functools.partial(before_halving, i), functools.partial(halving_stage, i)) for i in range(halvings)]
    state = [[] for _ in batches]
    cross_stages = [(nothing_before, spread_stage), (before_cross, cross_stage)]
    crossing = [list(pieces[:n]), list(pieces[n:])]
    blocks = ancestor.reshape(slot_count, n, g, sub, col_slots * width)
    shared = [blocks] * (g - 1)
    half = width // g
    quarter = half // n

    def core_sum(shares):
        share = shares[0]
        for k in range(1, g):
            share = share + along_core(shares[k], k)
        return share

    def plane_sum(share):
        cut = [lax.dynamic_slice_in_dim(share, (r ^ k) * quarter, quarter, 1) for k in range(n)]
        return tree_sum([cut[0]] + [along_row(cut[k], k) for k in range(1, n)])

    def plane_diag(shares):
        return plane_sum(core_sum(shares))

    def line_sum(part):
        return tree_sum([part] + [along_z(part, m) for m in range(1, n)])

    def plane_gather(part):
        parts = [part] + [along_row(part, k) for k in range(1, n)]
        return jnp.concatenate([pick(parts, r ^ j) for j in range(n)], axis=1)

    def core_gather(mine):
        halves = [mine] + [along_core(mine, k) for k in range(1, g)]
        return jnp.concatenate([pick(halves, c ^ j) for j in range(g)], axis=1)

    def joined(shares):
        return [jnp.concatenate([held[k] for held in shares]) for k in range(g)]

    def finish(b, off, with_off, with_diag):
        start, count = starts[b], batches[b]
        of_node = lambda i, ids, table: (start + i, 0, 0, 0)
        of_dest = lambda level: lambda i, ids, table: (ids[1] >> level, i, 0, 0)
        out_shape, out_specs = [], []
        if with_off:
            out_shape.append(jax.ShapeDtypeStruct((node_count, slot_count, sub, width), F32))
            out_specs.append(pl.BlockSpec((1, slot_count, sub, width), of_node))
        if with_diag:
            out_shape += [jax.ShapeDtypeStruct((count, half, width), F32)] * g
            out_specs += [pl.BlockSpec((1, half, width), lambda i, ids, table: (i, 0, 0))] * g
        result = pl.pallas_call(
            functools.partial(finish_kernel, g, halvings, with_off, with_diag, start),
            out_shape=out_shape,
            grid_spec=pltpu.PrefetchScalarGridSpec(
                num_scalar_prefetch=2,
                grid=(count,),
                in_specs=[pl.BlockSpec((1, CAP, sub, width), of_dest(level)) for level in levels]
                + [
                    pl.BlockSpec((1, CAP, sub, width), of_node),
                    pl.BlockSpec((1, width, width), lambda i, ids, table: (start + i, 0, 0)),
                ]
                + [pl.BlockSpec(memory_space=pl.ANY)] * (off is not None),
                out_specs=out_specs,
                scratch_shapes=[pltpu.VMEM((CAP, sub, width), F32)],
            ),
            input_output_aliases={} if off is None else {5 + halvings: 0},
            compiler_params=params,
            cost_estimate=pl.CostEstimate(flops=1, bytes_accessed=1, transcendentals=0),
            name="finish",
        )(ids, table, *state[b], packed, dinv, *([] if off is None else [off]))
        return result[0], list(result[with_off:])

    def last_diag():
        count, total = batches[-1], batches[-1] * CAP
        block = (node_count - count) // count
        of_dest = lambda level: lambda i, ids: (ids[1] >> level, 0, 0, 0)
        return pl.pallas_call(
            functools.partial(last_diag_kernel, g, halvings),
            out_shape=[jax.ShapeDtypeStruct((count, half, width), F32)] * g,
            grid_spec=pltpu.PrefetchScalarGridSpec(
                num_scalar_prefetch=1,
                grid=(1,),
                in_specs=[pl.BlockSpec((1, total, sub, width), of_dest(level)) for level in levels]
                + [
                    pl.BlockSpec((count, CAP, sub, width), lambda i, ids: (block, 0, 0, 0)),
                    pl.BlockSpec((count, width, width), lambda i, ids: (block, 0, 0)),
                ],
                out_specs=[pl.BlockSpec((count, half, width), lambda i, ids: (0, 0, 0))] * g,
            ),
            compiler_params=params,
            cost_estimate=pl.CostEstimate(flops=1, bytes_accessed=1, transcendentals=0),
            name="last_diag",
        )(ids, *state[last], packed, dinv)

    off, early, first_diag = None, [], None
    last = len(batches) - 1
    for phase in range(2 + len(stages) + last):
        done = phase - 2 - len(stages)
        now = [(b, phase - 2 - b) for b in range(last + 1) if 0 <= phase - 2 - b < len(stages)]
        now_crossing = [(group, phase - group) for group in range(2) if 0 <= phase - group < 2]
        for b, stage in now:
            if stage == 0:
                at = 0 if b == 0 else (starts[b] - batches[0]) * CAP
                state[b] = [array[at : at + batches[b] * CAP] for array in crossing[min(b, 1)]]
            state[b] = stages[stage][0](b, state[b])
        for group, stage in now_crossing:
            crossing[group] = cross_stages[stage][0](group, crossing[group])
        state, crossing, shared, early = after((state, crossing, shared, early))
        for b, stage in now:
            state[b] = stages[stage][1](b, state[b])
        for group, stage in now_crossing:
            crossing[group] = cross_stages[stage][1](group, crossing[group])
        if phase == 0:
            shared = [lax.dynamic_index_in_dim(shared[k - 1], c ^ k, 2, keepdims=False) for k in range(1, g)]
        elif phase == 1:
            shared = [along_core(shared[k - 1], k) for k in range(1, g)]
        if done == 0:
            off, shares = finish(0, None, True, True)
            early = [shares]
            state[0] = []
        elif done == 1:
            first_diag = plane_diag(joined(early))
            off, more = finish(1, off, True, True)
            state[1] = early = []
            state, first_diag, off, more = after((state, first_diag, off, more))
            break
        state, crossing, shared, early = after((state, crossing, shared, early))
    shares = last_diag()
    off, _ = finish(last, off, True, False)
    first = line_sum(first_diag)
    second = core_sum([jnp.concatenate(pair) for pair in zip(more, shares)])
    first, second = plane_gather(first), plane_sum(second)
    second, off = after((second, off))
    first, second = core_gather(first), line_sum(second)
    return off, jnp.concatenate([first, core_gather(plane_gather(second))], axis=0)


def solution(mesh):
    in_specs = (P("row", "col"), P(None, "row", "col", None), P(), P(), P())
    out_specs = (P(None, "row", "col", None), P())
    return jax.shard_map(body, mesh=mesh, in_specs=in_specs, out_specs=out_specs, check_vma=False)
```

```python
import functools

import jax
import jax.numpy as jnp
from jax import lax
from jax.experimental import pallas as pl
from jax.experimental.pallas import tpu as pltpu
from jax.sharding import PartitionSpec as P

CAP = 6
BATCHES = (2, 2, 2)
F32 = jnp.float32
BF16 = jnp.bfloat16
VMEM_LIMIT = 60 * 1024 * 1024
PRODUCT_VMEM = 56 * 1024 * 1024

COUNT, SLOT = 0, 1
RUN_COUNT, RUN_SLOT = SLOT + CAP + 1, SLOT + CAP + 2
PLACE = RUN_SLOT + CAP + 1


def split(x):
    high = x.astype(BF16)
    return high, (x - high.astype(F32)).astype(BF16)


def dot3(a, b, dims):
    left = jnp.concatenate([a[0], a[1], a[0]], axis=dims[0][0])
    right = jnp.concatenate([b[0], b[0], b[1]], axis=dims[1][0])
    return lax.dot_general(left, right, dimension_numbers=(dims, ((), ())), preferred_element_type=F32)


def prepare_kernel(n, g, groups, ids, structure, block_slot, panel, dinv, table, packed, *rest):
    pieces, gathered = rest[:-1], rest[-1]
    r, z, c = ids[0], ids[1], ids[2]
    node_count, slot_count, sub, width = panel.shape
    piece = sub // n
    place = [(b, i) for b, count in enumerate(groups) for i in range(count)]
    for s in range(node_count):
        row_bits = jnp.int32(0)
        col_bits = jnp.int32(0)
        for k in range(structure.shape[1]):
            slot = block_slot[structure[s, k]]
            for which in range(2):
                at = slot - (r, z)[which] * slot_count
                inside = (at >= 0) & (at < slot_count)
                bit = jnp.where(inside, jnp.left_shift(jnp.int32(1), jnp.where(inside, at, 0)), 0)
                if which == 0:
                    row_bits = row_bits | bit
                else:
                    col_bits = col_bits | bit
        counts = []
        for bits, first in ((row_bits, SLOT), (col_bits, RUN_SLOT)):
            for k in range(CAP + 1):
                table[s, first + k] = 0
            count = jnp.int32(0)
            for q in range(slot_count):
                bit = (bits >> q) & 1
                table[s, first + jnp.minimum(count, CAP)] = q
                if first == SLOT:
                    table[s, PLACE + q] = jnp.where(bit == 1, count, -1)
                count = count + bit
            table[s, first - 1] = count
            counts.append(count)
        count = counts[0]
        for k in range(CAP):
            gathered[pl.ds(k * sub, sub), :] = jnp.where(k < count, panel[s, table[s, SLOT + k]], 0.0)
        rows = dot3(split(gathered[...]), split(dinv[s]), ((1,), (0,))).reshape(CAP, sub, width)
        packed[s] = rows
        b, i = place[s]
        for k in range(n):
            part = rows[:, :piece]
            for j in range(1, n):
                part = jnp.where((r ^ k) == j, rows[:, j * piece : (j + 1) * piece], part)
            pieces[b * n + k][pl.ds(i * CAP, CAP)] = part


def product_kernel(n, g, start, ids, table, *rest):
    sources, near, far, (keep, send) = rest[:g], rest[g : g + n], rest[g + n : 2 * g + n - 1], rest[2 * g + n - 1 : 2 * g + n + 1]
    blocks, run, acc, sems, run_sems = rest[2 * g + n + 1 :]
    r, z, c = ids[0], ids[1], ids[2]
    node_count = blocks.shape[0]
    sub = blocks.shape[-2]
    width = acc.shape[-1]
    col_slots = sources[0].shape[-1] // width
    tall = n * sub

    def copy(i, j, k, which):
        slot = table[start + i, RUN_SLOT + j]
        cols = pl.ds(pl.multiple_of((slot % col_slots) * width, width), width)
        q = table[start + i, SLOT + k]
        source = sources[0].at[q, :, c, :, cols] if which == 0 else sources[which].at[q, :, :, cols]
        return pltpu.make_async_copy(source, blocks.at[i, j, k], sems.at[i, j, k])

    def begin(i, j, k):
        owner = table[start + i, RUN_SLOT + j] // col_slots
        for which in range(g):

            @pl.when((c ^ owner) == which)
            def _():
                copy(i, j, k, which).start()

    pieces = [
        pltpu.make_async_copy(far[kc - 1].at[jk] if kc else near[jk], run.at[:, c ^ kc, r ^ jk], run_sems.at[jk * g + kc])
        for jk in range(n)
        for kc in range(g)
    ]
    for piece in pieces:
        piece.start()
    for i in range(node_count):

        def column_blocks(j, _):
            lax.fori_loop(0, table[start + i, COUNT], lambda k, _: begin(i, j, k), None)

        lax.fori_loop(0, table[start + i, RUN_COUNT], column_blocks, None)
    for piece in pieces:
        piece.wait()

    for i in range(node_count):
        rows, columns = table[start + i, COUNT], table[start + i, RUN_COUNT]

        def column(j, _):
            high, low = split(run[:, :, :, i * CAP + j].reshape(width, width))
            right = jnp.concatenate([high, high, low], axis=0)
            lax.fori_loop(0, rows, lambda k, _: copy(i, j, k, 0).wait(), None)
            for few, many in ((0, 2), (2, 4), (4, CAP)):

                @pl.when((rows > few) & (rows <= many))
                def _():
                    high, low = split(blocks[i, j, :many].reshape(many * tall, width))
                    left = jnp.concatenate([high, low, high], axis=1)
                    value = jnp.dot(left, right, preferred_element_type=F32)
                    at = pl.ds(0, many * tall)
                    acc[at] = jnp.where(j == 0, value, acc[at] + value)

        lax.fori_loop(0, columns, column, None)
        for k in range(CAP):
            live = (k < rows) & (columns > 0)
            for h in range(n // 2):
                even, odd = [
                    jnp.where(live, acc[pl.ds((k * n + 2 * h + bit) * sub, sub)], 0.0) for bit in range(2)
                ]
                keep[h, i * CAP + k] = jnp.where((z & 1) == 0, even, odd)
                send[h, i * CAP + k] = jnp.where((z & 1) == 0, odd, even)


def finish_kernel(g, halvings, with_off, with_diag, start, ids, table, base, *rest):
    received, packed, dinv = rest[:halvings], rest[halvings], rest[halvings + 1]
    product, outs = rest[-1], rest[-1 - with_off - g * with_diag : -1]
    s = start + pl.program_id(0)
    total = base[0]
    for more in received:
        total = total + more[0]
    product[...] = total
    sub, width = product.shape[1:]
    if with_off:
        off = outs[0]
        for q in range(off.shape[1]):
            at = table[s, PLACE + q]
            block = product[jnp.maximum(at, 0)]
            off[0, q] = jnp.where(at >= 0, -block, 0.0)
    if not with_diag:
        return
    mine = packed[0].reshape(CAP * sub, width)
    diag = dot3(split(mine), split(product[...].reshape(CAP * sub, width)), ((0,), (0,)))
    store_shares(diag, dinv, g, ids, outs[with_off:])


def store_shares(diag, dinv, g, ids, shares):
    def store(value):
        half = value.shape[0] // g
        for kc in range(g):
            part = value[:half]
            for j in range(1, g):
                part = jnp.where((ids[2] ^ kc) == j, value[j * half : (j + 1) * half], part)
            shares[kc][0] = part

    store(diag)

    @pl.when((ids[0] == 0) & (ids[1] == 0) & (ids[2] == 0))
    def _():
        factor = split(dinv[0])
        store(diag + dot3(factor, factor, ((0,), (0,))))


def last_diag_kernel(g, halvings, ids, base, *rest):
    received, packed, dinv, shares = rest[:halvings], rest[halvings], rest[halvings + 1], rest[halvings + 2 :]
    width = dinv.shape[-1]
    half = width // g
    dims = ((0,), (0,))
    for i in range(dinv.shape[0]):
        at = pl.ds(i * CAP, CAP)
        total = base[0, at]
        for more in received:
            total = total + more[0, at]
        diag = dot3(split(packed[i].reshape(-1, width)), split(total.reshape(-1, width)), dims)

        def store(value):
            for kc in range(g):
                part = value[:half]
                for j in range(1, g):
                    part = jnp.where((ids[2] ^ kc) == j, value[j * half : (j + 1) * half], part)
                shares[kc][i] = part

        store(diag)

        @pl.when((ids[0] == 0) & (ids[1] == 0) & (ids[2] == 0))
        def _():
            factor = split(dinv[i])
            store(diag + dot3(factor, factor, dims))


def tree_sum(terms):
    while len(terms) > 1:
        terms = [terms[i] + terms[i + 1] for i in range(0, len(terms), 2)]
    return terms[0]


def pick(arrays, index):
    value = arrays[0]
    for k in range(1, len(arrays)):
        value = jnp.where(index == k, arrays[k], value)
    return value


def after(x):
    return lax.optimization_barrier(x)


def body(ancestor, panel, dinv, structure, block_slot):
    n = lax.axis_size("row")
    g = lax.axis_size("col") // n
    r = lax.axis_index("row")
    col = lax.axis_index("col")
    z, c = col // g, col % g
    node_count, slot_count, sub, width = panel.shape
    col_slots = slot_count // g
    piece = sub // n
    ids = jnp.stack([r, z, c]).astype(jnp.int32)
    table_width = PLACE + slot_count
    batches = BATCHES
    groups = (batches[0], sum(batches[1:]))
    smem = pl.BlockSpec(memory_space=pltpu.SMEM)
    vmem = pl.BlockSpec(memory_space=pltpu.VMEM)
    params = pltpu.CompilerParams(vmem_limit_bytes=VMEM_LIMIT)

    def along_row(x, k):
        return lax.ppermute(x, "row", [(i, i ^ k) for i in range(n)])

    def along_z(x, m):
        return lax.ppermute(x, "col", [(i * g + j, (i ^ m) * g + j) for i in range(n) for j in range(g)])

    def along_core(x, k):
        return lax.ppermute(x, "col", [(i * g + j, i * g + (j ^ k)) for i in range(n) for j in range(g)])

    out = pl.pallas_call(
        functools.partial(prepare_kernel, n, g, groups),
        out_shape=[
            jax.ShapeDtypeStruct((node_count, table_width), jnp.int32),
            jax.ShapeDtypeStruct((node_count, CAP, sub, width), F32),
        ]
        + [jax.ShapeDtypeStruct((count * CAP, piece, width), F32) for count in groups for _ in range(n)],
        in_specs=[smem, smem, smem, vmem, vmem],
        out_specs=[smem] + [vmem] * (1 + n * len(groups)),
        scratch_shapes=[pltpu.VMEM((CAP * sub, width), F32)],
        compiler_params=params,
        name="prepare",
    )(ids, structure, block_slot, panel, dinv)
    table, packed, pieces = out[0], out[1], out[2:]

    starts = [sum(batches[:b]) for b in range(len(batches))]
    halvings = n.bit_length() - 1

    def nothing_before(b, held):
        return held

    def spread_stage(b, own):
        return [own[0]] + [along_row(own[k], k) for k in range(1, n)]

    def before_cross(b, spread):
        return [pick(spread, r ^ z ^ m) for m in range(n)]

    def cross_stage(b, got):
        return [got[0]] + [along_z(got[m], m) for m in range(1, n)]

    def before_plane(b, got):
        return [jnp.stack([pick(got, z ^ i) for i in range(n)])]

    def plane_stage(b, run):
        return run + [along_row(run[0], k) for k in range(1, n)]

    def product_stage(b, plane):
        start, count = starts[b], batches[b]
        total = count * CAP
        parts = list(plane) + [along_core(jnp.stack(plane), k) for k in range(1, g)]
        return pl.pallas_call(
            functools.partial(product_kernel, n, g, start),
            out_shape=[jax.ShapeDtypeStruct((n // 2, total, sub, width), F32)] * 2,
            in_specs=[smem, smem] + [pl.BlockSpec(memory_space=pltpu.HBM)] * (2 * g + n - 1),
            out_specs=[vmem] * 2,
            scratch_shapes=[
                pltpu.VMEM((count, CAP, CAP, n, sub, width), F32),
                pltpu.VMEM((n, g, n, total, piece, width), F32),
                pltpu.VMEM((CAP * n * sub, width), F32),
                pltpu.SemaphoreType.DMA((count, CAP, CAP)),
                pltpu.SemaphoreType.DMA((n * g,)),
            ],
            compiler_params=pltpu.CompilerParams(vmem_limit_bytes=PRODUCT_VMEM),
            cost_estimate=pl.CostEstimate(flops=1, bytes_accessed=1, transcendentals=0),
            name="product",
        )(ids, table, blocks, *shared, *parts)

    levels = [1] + list(range(1, halvings + 1))

    def before_halving(i, b, held):
        if i == 0:
            return held
        high, bit = n >> (i + 1), (z >> i) & 1
        send = None
        for level, array in zip(levels, held):
            inner = 1 << (i - level)
            split_up = array.reshape((high, 2, inner) + array.shape[1:])
            start_at = (0, 1 - bit, (z >> level) & (inner - 1)) + (0,) * (array.ndim - 1)
            part = lax.dynamic_slice(split_up, start_at, (high, 1, 1) + array.shape[1:])
            part = part.reshape((high,) + array.shape[1:])
            send = part if send is None else send + part
        return list(held) + [send]

    def halving_stage(i, b, held):
        return list(held[:-1]) + [along_z(held[-1], 1 << i)]

    stages = [
        (before_plane, plane_stage),
        (nothing_before, product_stage),
    ]
    stages += [(functools.partial(before_halving, i), functools.partial(halving_stage, i)) for i in range(halvings)]
    state = [[] for _ in batches]
    cross_stages = [(nothing_before, spread_stage), (before_cross, cross_stage)]
    crossing = [list(pieces[:n]), list(pieces[n:])]
    blocks = ancestor.reshape(slot_count, n, g, sub, col_slots * width)
    shared = [blocks] * (g - 1)
    half = width // g
    quarter = half // n

    def core_sum(shares):
        share = shares[0]
        for k in range(1, g):
            share = share + along_core(shares[k], k)
        return share

    def plane_sum(share):
        cut = [lax.dynamic_slice_in_dim(share, (r ^ k) * quarter, quarter, 1) for k in range(n)]
        return tree_sum([cut[0]] + [along_row(cut[k], k) for k in range(1, n)])

    def plane_diag(shares):
        return plane_sum(core_sum(shares))

    def line_sum(part):
        return tree_sum([part] + [along_z(part, m) for m in range(1, n)])

    def plane_gather(part):
        parts = [part] + [along_row(part, k) for k in range(1, n)]
        return jnp.concatenate([pick(parts, r ^ j) for j in range(n)], axis=1)

    def core_gather(mine):
        halves = [mine] + [along_core(mine, k) for k in range(1, g)]
        return jnp.concatenate([pick(halves, c ^ j) for j in range(g)], axis=1)

    def joined(shares):
        return [jnp.concatenate([held[k] for held in shares]) for k in range(g)]

    def finish(b, off, with_off, with_diag):
        start, count = starts[b], batches[b]
        of_node = lambda i, ids, table: (start + i, 0, 0, 0)
        of_dest = lambda level: lambda i, ids, table: (ids[1] >> level, i, 0, 0)
        out_shape, out_specs = [], []
        if with_off:
            out_shape.append(jax.ShapeDtypeStruct((node_count, slot_count, sub, width), F32))
            out_specs.append(pl.BlockSpec((1, slot_count, sub, width), of_node))
        if with_diag:
            out_shape += [jax.ShapeDtypeStruct((count, half, width), F32)] * g
            out_specs += [pl.BlockSpec((1, half, width), lambda i, ids, table: (i, 0, 0))] * g
        result = pl.pallas_call(
            functools.partial(finish_kernel, g, halvings, with_off, with_diag, start),
            out_shape=out_shape,
            grid_spec=pltpu.PrefetchScalarGridSpec(
                num_scalar_prefetch=2,
                grid=(count,),
                in_specs=[pl.BlockSpec((1, CAP, sub, width), of_dest(level)) for level in levels]
                + [
                    pl.BlockSpec((1, CAP, sub, width), of_node),
                    pl.BlockSpec((1, width, width), lambda i, ids, table: (start + i, 0, 0)),
                ]
                + [pl.BlockSpec(memory_space=pl.ANY)] * (off is not None),
                out_specs=out_specs,
                scratch_shapes=[pltpu.VMEM((CAP, sub, width), F32)],
            ),
            input_output_aliases={} if off is None else {5 + halvings: 0},
            compiler_params=params,
            cost_estimate=pl.CostEstimate(flops=1, bytes_accessed=1, transcendentals=0),
            name="finish",
        )(ids, table, *state[b], packed, dinv, *([] if off is None else [off]))
        return result[0], list(result[with_off:])

    def last_diag():
        count, total = batches[-1], batches[-1] * CAP
        block = (node_count - count) // count
        of_dest = lambda level: lambda i, ids: (ids[1] >> level, 0, 0, 0)
        return pl.pallas_call(
            functools.partial(last_diag_kernel, g, halvings),
            out_shape=[jax.ShapeDtypeStruct((count, half, width), F32)] * g,
            grid_spec=pltpu.PrefetchScalarGridSpec(
                num_scalar_prefetch=1,
                grid=(1,),
                in_specs=[pl.BlockSpec((1, total, sub, width), of_dest(level)) for level in levels]
                + [
                    pl.BlockSpec((count, CAP, sub, width), lambda i, ids: (block, 0, 0, 0)),
                    pl.BlockSpec((count, width, width), lambda i, ids: (block, 0, 0)),
                ],
                out_specs=[pl.BlockSpec((count, half, width), lambda i, ids: (0, 0, 0))] * g,
            ),
            compiler_params=params,
            cost_estimate=pl.CostEstimate(flops=1, bytes_accessed=1, transcendentals=0),
            name="last_diag",
        )(ids, *state[last], packed, dinv)

    off, early, first_diag = None, [], None
    last = len(batches) - 1
    for phase in range(2 + len(stages) + last):
        done = phase - 2 - len(stages)
        now = [(b, phase - 2 - b) for b in range(last + 1) if 0 <= phase - 2 - b < len(stages)]
        now_crossing = [(group, phase - group) for group in range(2) if 0 <= phase - group < 2]
        for b, stage in now:
            if stage == 0:
                at = 0 if b == 0 else (starts[b] - batches[0]) * CAP
                state[b] = [array[at : at + batches[b] * CAP] for array in crossing[min(b, 1)]]
            state[b] = stages[stage][0](b, state[b])
        for group, stage in now_crossing:
            crossing[group] = cross_stages[stage][0](group, crossing[group])
        state, crossing, shared, early = after((state, crossing, shared, early))
        for b, stage in now:
            state[b] = stages[stage][1](b, state[b])
        for group, stage in now_crossing:
            crossing[group] = cross_stages[stage][1](group, crossing[group])
        if phase == 0:
            shared = [lax.dynamic_index_in_dim(shared[k - 1], c ^ k, 2, keepdims=False) for k in range(1, g)]
        elif phase == 1:
            shared = [along_core(shared[k - 1], k) for k in range(1, g)]
        if done == 0:
            off, shares = finish(0, None, True, True)
            early = [shares]
            state[0] = []
        elif done == 1:
            first_diag = plane_diag(joined(early))
            off, more = finish(1, off, True, True)
            state[1] = early = []
            state, first_diag, off, more = after((state, first_diag, off, more))
            break
        state, crossing, shared, early = after((state, crossing, shared, early))
    shares = last_diag()
    off, _ = finish(last, off, True, False)
    first = line_sum(first_diag)
    second = core_sum([jnp.concatenate(pair) for pair in zip(more, shares)])
    first, second = plane_gather(first), plane_sum(second)
    second, off = after((second, off))
    first, second = core_gather(first), line_sum(second)
    return off, jnp.concatenate([first, core_gather(plane_gather(second))], axis=0)


def solution(mesh):
    in_specs = (P("row", "col"), P(None, "row", "col", None), P(), P(), P())
    out_specs = (P(None, "row", "col", None), P())
    return jax.shard_map(body, mesh=mesh, in_specs=in_specs, out_specs=out_specs, check_vma=False)
```

```python
import functools

import jax
import jax.numpy as jnp
from jax import lax
from jax.experimental import pallas as pl
from jax.experimental.pallas import tpu as pltpu
from jax.sharding import PartitionSpec as P

CAP = 6
BATCHES = (2, 2, 2)
F32 = jnp.float32
BF16 = jnp.bfloat16
VMEM_LIMIT = 60 * 1024 * 1024
PRODUCT_VMEM = 56 * 1024 * 1024

COUNT, SLOT = 0, 1
RUN_COUNT, RUN_SLOT = SLOT + CAP + 1, SLOT + CAP + 2
PLACE = RUN_SLOT + CAP + 1


def split(x):
    high = x.astype(BF16)
    return high, (x - high.astype(F32)).astype(BF16)


def dot3(a, b, dims):
    left = jnp.concatenate([a[0], a[1], a[0]], axis=dims[0][0])
    right = jnp.concatenate([b[0], b[0], b[1]], axis=dims[1][0])
    return lax.dot_general(left, right, dimension_numbers=(dims, ((), ())), preferred_element_type=F32)


def prepare_kernel(n, g, groups, ids, structure, block_slot, panel, dinv, table, packed, *rest):
    pieces, gathered = rest[:-1], rest[-1]
    r, z, c = ids[0], ids[1], ids[2]
    node_count, slot_count, sub, width = panel.shape
    piece = sub // n
    place = [(b, i) for b, count in enumerate(groups) for i in range(count)]
    for s in range(node_count):
        row_bits = jnp.int32(0)
        col_bits = jnp.int32(0)
        for k in range(structure.shape[1]):
            slot = block_slot[structure[s, k]]
            for which in range(2):
                at = slot - (r, z)[which] * slot_count
                inside = (at >= 0) & (at < slot_count)
                bit = jnp.where(inside, jnp.left_shift(jnp.int32(1), jnp.where(inside, at, 0)), 0)
                if which == 0:
                    row_bits = row_bits | bit
                else:
                    col_bits = col_bits | bit
        counts = []
        for bits, first in ((row_bits, SLOT), (col_bits, RUN_SLOT)):
            for k in range(CAP + 1):
                table[s, first + k] = 0
            count = jnp.int32(0)
            for q in range(slot_count):
                bit = (bits >> q) & 1
                table[s, first + jnp.minimum(count, CAP)] = q
                if first == SLOT:
                    table[s, PLACE + q] = jnp.where(bit == 1, count, -1)
                count = count + bit
            table[s, first - 1] = count
            counts.append(count)
        count = counts[0]
        for k in range(CAP):
            gathered[pl.ds(k * sub, sub), :] = jnp.where(k < count, panel[s, table[s, SLOT + k]], 0.0)
        rows = dot3(split(gathered[...]), split(dinv[s]), ((1,), (0,))).reshape(CAP, sub, width)
        packed[s] = rows
        b, i = place[s]
        for k in range(n):
            part = rows[:, :piece]
            for j in range(1, n):
                part = jnp.where((r ^ k) == j, rows[:, j * piece : (j + 1) * piece], part)
            pieces[b * n + k][pl.ds(i * CAP, CAP)] = part


def product_kernel(n, g, start, ids, table, *rest):
    sources, near, far, (keep, send) = rest[:g], rest[g : g + n], rest[g + n : 2 * g + n - 1], rest[2 * g + n - 1 : 2 * g + n + 1]
    blocks, run, acc, sems, run_sems = rest[2 * g + n + 1 :]
    r, z, c = ids[0], ids[1], ids[2]
    node_count = blocks.shape[0]
    sub = blocks.shape[-2]
    width = acc.shape[-1]
    col_slots = sources[0].shape[-1] // width
    tall = n * sub

    def copy(i, j, k, which):
        slot = table[start + i, RUN_SLOT + j]
        cols = pl.ds(pl.multiple_of((slot % col_slots) * width, width), width)
        q = table[start + i, SLOT + k]
        source = sources[0].at[q, :, c, :, cols] if which == 0 else sources[which].at[q, :, :, cols]
        return pltpu.make_async_copy(source, blocks.at[i, j, k], sems.at[i, j, k])

    def begin(i, j, k):
        owner = table[start + i, RUN_SLOT + j] // col_slots
        for which in range(g):

            @pl.when((c ^ owner) == which)
            def _():
                copy(i, j, k, which).start()

    pieces = [
        pltpu.make_async_copy(far[kc - 1].at[jk] if kc else near[jk], run.at[:, c ^ kc, r ^ jk], run_sems.at[jk * g + kc])
        for jk in range(n)
        for kc in range(g)
    ]
    for piece in pieces:
        piece.start()
    for i in range(node_count):

        def column_blocks(j, _):
            lax.fori_loop(0, table[start + i, COUNT], lambda k, _: begin(i, j, k), None)

        lax.fori_loop(0, table[start + i, RUN_COUNT], column_blocks, None)
    for piece in pieces:
        piece.wait()

    for i in range(node_count):
        rows, columns = table[start + i, COUNT], table[start + i, RUN_COUNT]

        def column(j, _):
            high, low = split(run[:, :, :, i * CAP + j].reshape(width, width))
            right = jnp.concatenate([high, high, low], axis=0)
            lax.fori_loop(0, rows, lambda k, _: copy(i, j, k, 0).wait(), None)
            for few, many in ((0, 2), (2, 4), (4, CAP)):

                @pl.when((rows > few) & (rows <= many))
                def _():
                    high, low = split(blocks[i, j, :many].reshape(many * tall, width))
                    left = jnp.concatenate([high, low, high], axis=1)
                    value = jnp.dot(left, right, preferred_element_type=F32)
                    at = pl.ds(0, many * tall)
                    acc[at] = jnp.where(j == 0, value, acc[at] + value)

        lax.fori_loop(0, columns, column, None)
        for k in range(CAP):
            live = (k < rows) & (columns > 0)
            for h in range(n // 2):
                even, odd = [
                    jnp.where(live, acc[pl.ds((k * n + 2 * h + bit) * sub, sub)], 0.0) for bit in range(2)
                ]
                keep[h, i * CAP + k] = jnp.where((z & 1) == 0, even, odd)
                send[h, i * CAP + k] = jnp.where((z & 1) == 0, odd, even)


def finish_kernel(g, halvings, with_off, with_diag, start, ids, table, base, *rest):
    received, packed, dinv = rest[:halvings], rest[halvings], rest[halvings + 1]
    product, outs = rest[-1], rest[-1 - with_off - g * with_diag : -1]
    s = start + pl.program_id(0)
    total = base[0]
    for more in received:
        total = total + more[0]
    product[...] = total
    sub, width = product.shape[1:]
    if with_off:
        off = outs[0]
        for q in range(off.shape[1]):
            at = table[s, PLACE + q]
            block = product[jnp.maximum(at, 0)]
            off[0, q] = jnp.where(at >= 0, -block, 0.0)
    if not with_diag:
        return
    mine = packed[0].reshape(CAP * sub, width)
    diag = dot3(split(mine), split(product[...].reshape(CAP * sub, width)), ((0,), (0,)))
    store_shares(diag, dinv, g, ids, outs[with_off:])


def store_shares(diag, dinv, g, ids, shares):
    def store(value):
        half = value.shape[0] // g
        for kc in range(g):
            part = value[:half]
            for j in range(1, g):
                part = jnp.where((ids[2] ^ kc) == j, value[j * half : (j + 1) * half], part)
            shares[kc][0] = part

    store(diag)

    @pl.when((ids[0] == 0) & (ids[1] == 0) & (ids[2] == 0))
    def _():
        factor = split(dinv[0])
        store(diag + dot3(factor, factor, ((0,), (0,))))


def last_diag_kernel(g, halvings, ids, base, *rest):
    received, packed, dinv, shares = rest[:halvings], rest[halvings], rest[halvings + 1], rest[halvings + 2 :]
    width = dinv.shape[-1]
    half = width // g
    dims = ((0,), (0,))
    for i in range(dinv.shape[0]):
        at = pl.ds(i * CAP, CAP)
        total = base[0, at]
        for more in received:
            total = total + more[0, at]
        diag = dot3(split(packed[i].reshape(-1, width)), split(total.reshape(-1, width)), dims)

        def store(value):
            for kc in range(g):
                part = value[:half]
                for j in range(1, g):
                    part = jnp.where((ids[2] ^ kc) == j, value[j * half : (j + 1) * half], part)
                shares[kc][i] = part

        store(diag)

        @pl.when((ids[0] == 0) & (ids[1] == 0) & (ids[2] == 0))
        def _():
            factor = split(dinv[i])
            store(diag + dot3(factor, factor, dims))


def tree_sum(terms):
    while len(terms) > 1:
        terms = [terms[i] + terms[i + 1] for i in range(0, len(terms), 2)]
    return terms[0]


def pick(arrays, index):
    value = arrays[0]
    for k in range(1, len(arrays)):
        value = jnp.where(index == k, arrays[k], value)
    return value


def after(x):
    return lax.optimization_barrier(x)


def body(ancestor, panel, dinv, structure, block_slot):
    n = lax.axis_size("row")
    g = lax.axis_size("col") // n
    r = lax.axis_index("row")
    col = lax.axis_index("col")
    z, c = col // g, col % g
    node_count, slot_count, sub, width = panel.shape
    col_slots = slot_count // g
    piece = sub // n
    ids = jnp.stack([r, z, c]).astype(jnp.int32)
    table_width = PLACE + slot_count
    batches = BATCHES
    groups = (batches[0], sum(batches[1:]))
    smem = pl.BlockSpec(memory_space=pltpu.SMEM)
    vmem = pl.BlockSpec(memory_space=pltpu.VMEM)
    params = pltpu.CompilerParams(vmem_limit_bytes=VMEM_LIMIT)

    def along_row(x, k):
        return lax.ppermute(x, "row", [(i, i ^ k) for i in range(n)])

    def along_z(x, m):
        return lax.ppermute(x, "col", [(i * g + j, (i ^ m) * g + j) for i in range(n) for j in range(g)])

    def along_core(x, k):
        return lax.ppermute(x, "col", [(i * g + j, i * g + (j ^ k)) for i in range(n) for j in range(g)])

    out = pl.pallas_call(
        functools.partial(prepare_kernel, n, g, groups),
        out_shape=[
            jax.ShapeDtypeStruct((node_count, table_width), jnp.int32),
            jax.ShapeDtypeStruct((node_count, CAP, sub, width), F32),
        ]
        + [jax.ShapeDtypeStruct((count * CAP, piece, width), F32) for count in groups for _ in range(n)],
        in_specs=[smem, smem, smem, vmem, vmem],
        out_specs=[smem] + [vmem] * (1 + n * len(groups)),
        scratch_shapes=[pltpu.VMEM((CAP * sub, width), F32)],
        compiler_params=params,
        name="prepare",
    )(ids, structure, block_slot, panel, dinv)
    table, packed, pieces = out[0], out[1], out[2:]

    starts = [sum(batches[:b]) for b in range(len(batches))]
    halvings = n.bit_length() - 1

    def nothing_before(b, held):
        return held

    def spread_stage(b, own):
        return [own[0]] + [along_row(own[k], k) for k in range(1, n)]

    def before_cross(b, spread):
        return [pick(spread, r ^ z ^ m) for m in range(n)]

    def cross_stage(b, got):
        return [got[0]] + [along_z(got[m], m) for m in range(1, n)]

    def before_plane(b, got):
        return [jnp.stack([pick(got, z ^ i) for i in range(n)])]

    def plane_stage(b, run):
        return run + [along_row(run[0], k) for k in range(1, n)]

    def product_stage(b, plane):
        start, count = starts[b], batches[b]
        total = count * CAP
        parts = list(plane) + [along_core(jnp.stack(plane), k) for k in range(1, g)]
        return pl.pallas_call(
            functools.partial(product_kernel, n, g, start),
            out_shape=[jax.ShapeDtypeStruct((n // 2, total, sub, width), F32)] * 2,
            in_specs=[smem, smem] + [pl.BlockSpec(memory_space=pltpu.HBM)] * (2 * g + n - 1),
            out_specs=[vmem] * 2,
            scratch_shapes=[
                pltpu.VMEM((count, CAP, CAP, n, sub, width), F32),
                pltpu.VMEM((n, g, n, total, piece, width), F32),
                pltpu.VMEM((CAP * n * sub, width), F32),
                pltpu.SemaphoreType.DMA((count, CAP, CAP)),
                pltpu.SemaphoreType.DMA((n * g,)),
            ],
            compiler_params=pltpu.CompilerParams(vmem_limit_bytes=PRODUCT_VMEM),
            cost_estimate=pl.CostEstimate(flops=1, bytes_accessed=1, transcendentals=0),
            name="product",
        )(ids, table, blocks, *shared, *parts)

    levels = [1] + list(range(1, halvings + 1))

    def before_halving(i, b, held):
        if i == 0:
            return held
        high, bit = n >> (i + 1), (z >> i) & 1
        send = None
        for level, array in zip(levels, held):
            inner = 1 << (i - level)
            split_up = array.reshape((high, 2, inner) + array.shape[1:])
            start_at = (0, 1 - bit, (z >> level) & (inner - 1)) + (0,) * (array.ndim - 1)
            part = lax.dynamic_slice(split_up, start_at, (high, 1, 1) + array.shape[1:])
            part = part.reshape((high,) + array.shape[1:])
            send = part if send is None else send + part
        return list(held) + [send]

    def halving_stage(i, b, held):
        return list(held[:-1]) + [along_z(held[-1], 1 << i)]

    stages = [
        (before_plane, plane_stage),
        (nothing_before, product_stage),
    ]
    stages += [(functools.partial(before_halving, i), functools.partial(halving_stage, i)) for i in range(halvings)]
    state = [[] for _ in batches]
    cross_stages = [(nothing_before, spread_stage), (before_cross, cross_stage)]
    crossing = [list(pieces[:n]), list(pieces[n:])]
    blocks = ancestor.reshape(slot_count, n, g, sub, col_slots * width)
    shared = [blocks] * (g - 1)
    half = width // g
    quarter = half // n

    def core_sum(shares):
        share = shares[0]
        for k in range(1, g):
            share = share + along_core(shares[k], k)
        return share

    def plane_sum(share):
        cut = [lax.dynamic_slice_in_dim(share, (r ^ k) * quarter, quarter, 1) for k in range(n)]
        return tree_sum([cut[0]] + [along_row(cut[k], k) for k in range(1, n)])

    def plane_diag(shares):
        return plane_sum(core_sum(shares))

    def line_sum(part):
        return tree_sum([part] + [along_z(part, m) for m in range(1, n)])

    def plane_gather(part):
        parts = [part] + [along_row(part, k) for k in range(1, n)]
        return jnp.concatenate([pick(parts, r ^ j) for j in range(n)], axis=1)

    def core_gather(mine):
        halves = [mine] + [along_core(mine, k) for k in range(1, g)]
        return jnp.concatenate([pick(halves, c ^ j) for j in range(g)], axis=1)

    def joined(shares):
        return [jnp.concatenate([held[k] for held in shares]) for k in range(g)]

    def finish(b, off, with_off, with_diag):
        start, count = starts[b], batches[b]
        of_node = lambda i, ids, table: (start + i, 0, 0, 0)
        of_dest = lambda level: lambda i, ids, table: (ids[1] >> level, i, 0, 0)
        out_shape, out_specs = [], []
        if with_off:
            out_shape.append(jax.ShapeDtypeStruct((node_count, slot_count, sub, width), F32))
            out_specs.append(pl.BlockSpec((1, slot_count, sub, width), of_node))
        if with_diag:
            out_shape += [jax.ShapeDtypeStruct((count, half, width), F32)] * g
            out_specs += [pl.BlockSpec((1, half, width), lambda i, ids, table: (i, 0, 0))] * g
        result = pl.pallas_call(
            functools.partial(finish_kernel, g, halvings, with_off, with_diag, start),
            out_shape=out_shape,
            grid_spec=pltpu.PrefetchScalarGridSpec(
                num_scalar_prefetch=2,
                grid=(count,),
                in_specs=[pl.BlockSpec((1, CAP, sub, width), of_dest(level)) for level in levels]
                + [
                    pl.BlockSpec((1, CAP, sub, width), of_node),
                    pl.BlockSpec((1, width, width), lambda i, ids, table: (start + i, 0, 0)),
                ]
                + [pl.BlockSpec(memory_space=pl.ANY)] * (off is not None),
                out_specs=out_specs,
                scratch_shapes=[pltpu.VMEM((CAP, sub, width), F32)],
            ),
            input_output_aliases={} if off is None else {5 + halvings: 0},
            compiler_params=params,
            cost_estimate=pl.CostEstimate(flops=1, bytes_accessed=1, transcendentals=0),
            name="finish",
        )(ids, table, *state[b], packed, dinv, *([] if off is None else [off]))
        return result[0], list(result[with_off:])

    def last_diag():
        count, total = batches[-1], batches[-1] * CAP
        block = (node_count - count) // count
        of_dest = lambda level: lambda i, ids: (ids[1] >> level, 0, 0, 0)
        return pl.pallas_call(
            functools.partial(last_diag_kernel, g, halvings),
            out_shape=[jax.ShapeDtypeStruct((count, half, width), F32)] * g,
            grid_spec=pltpu.PrefetchScalarGridSpec(
                num_scalar_prefetch=1,
                grid=(1,),
                in_specs=[pl.BlockSpec((1, total, sub, width), of_dest(level)) for level in levels]
                + [
                    pl.BlockSpec((count, CAP, sub, width), lambda i, ids: (block, 0, 0, 0)),
                    pl.BlockSpec((count, width, width), lambda i, ids: (block, 0, 0)),
                ],
                out_specs=[pl.BlockSpec((count, half, width), lambda i, ids: (0, 0, 0))] * g,
            ),
            compiler_params=params,
            cost_estimate=pl.CostEstimate(flops=1, bytes_accessed=1, transcendentals=0),
            name="last_diag",
        )(ids, *state[last], packed, dinv)

    off, early, first_diag = None, [], None
    last = len(batches) - 1
    for phase in range(2 + len(stages) + last):
        done = phase - 2 - len(stages)
        now = [(b, phase - 2 - b) for b in range(last + 1) if 0 <= phase - 2 - b < len(stages)]
        now_crossing = [(group, phase - group) for group in range(2) if 0 <= phase - group < 2]
        for b, stage in now:
            if stage == 0:
                at = 0 if b == 0 else (starts[b] - batches[0]) * CAP
                state[b] = [array[at : at + batches[b] * CAP] for array in crossing[min(b, 1)]]
            state[b] = stages[stage][0](b, state[b])
        for group, stage in now_crossing:
            crossing[group] = cross_stages[stage][0](group, crossing[group])
        state, crossing, shared, early = after((state, crossing, shared, early))
        for b, stage in now:
            state[b] = stages[stage][1](b, state[b])
        for group, stage in now_crossing:
            crossing[group] = cross_stages[stage][1](group, crossing[group])
        if phase == 1:
            shared = [lax.dynamic_index_in_dim(shared[k - 1], c ^ k, 2, keepdims=False) for k in range(1, g)]
        elif phase == 2:
            shared = [along_core(shared[k - 1], k) for k in range(1, g)]
        if done == 0:
            off, shares = finish(0, None, True, True)
            early = [shares]
            state[0] = []
        elif done == 1:
            first_diag = plane_diag(joined(early))
            off, more = finish(1, off, True, True)
            state[1] = early = []
            state, first_diag, off, more = after((state, first_diag, off, more))
            break
        state, crossing, shared, early = after((state, crossing, shared, early))
    shares = last_diag()
    off, _ = finish(last, off, True, False)
    first = line_sum(first_diag)
    second = core_sum([jnp.concatenate(pair) for pair in zip(more, shares)])
    first, second = plane_gather(first), plane_sum(second)
    second, off = after((second, off))
    first, second = core_gather(first), line_sum(second)
    return off, jnp.concatenate([first, core_gather(plane_gather(second))], axis=0)


def solution(mesh):
    in_specs = (P("row", "col"), P(None, "row", "col", None), P(), P(), P())
    out_specs = (P(None, "row", "col", None), P())
    return jax.shard_map(body, mesh=mesh, in_specs=in_specs, out_specs=out_specs, check_vma=False)
```
